512 devices in a mesh: fsdp: 64 (over z, x, core), rep: 8 (over y).
Axes of the slice: x: 4, y: 8, z: 8, core: 2. Of those that a mesh axis runs over, the one named last changes fastest.
Arguments:
- gradients: bfloat16 [8, 16, 256, 8192], P('rep', None, 'fsdp'), may hold values from -0.5 to 0.5
- owned_blocks: int32 [64, 8, 2], replicated, may hold values from 0 to 512, as said below
- rows_valid: int32 [512], replicated, may hold values from 128 to 256
- cols_valid: int32 [512], replicated, may hold values from 128 to 256
- left_factor: float32 [64, 8, 2, 256, 256], P('fsdp', 'rep'), may hold values from -3 to 3
- right_factor: float32 [64, 8, 2, 256, 256], P('fsdp', 'rep'), may hold values from -3 to 3
- left_root: bfloat16 [64, 8, 2, 256, 256], P('fsdp', 'rep'), may hold values from -1 to 3
- right_root: bfloat16 [64, 8, 2, 256, 256], P('fsdp', 'rep'), may hold values from -1 to 3
- second_moment: float32 [64, 8, 2, 256, 256], P('fsdp', 'rep'), may hold values from 0.0001 to 0.01
Outputs:
- update: bfloat16 [16, 256, 8192], P(None, 'fsdp')
- left_new: float32 [64, 8, 2, 256, 256], P('fsdp', 'rep')
- right_new: float32 [64, 8, 2, 256, 256], P('fsdp', 'rep')
The draws below stay inside these ranges and needn't reach their ends.
Inputs may be any that keep to these rules, and one draw needn't show every extreme that they name: `owned_blocks`: every block id 0 to 511 stands in exactly one slot; the value 512 marks an empty slot; slots of one owner are filled from slot 0; some owners fill all 2 slots and some hold none.
All inputs are finite; a program needn't handle non-finite values.
Results may differ from the reference program's by a relative error of at most 0.02.
Values may be sent and summed in bfloat16 or wider, within the bound.
No kernel may reach another device: no remote copies, remote signals or barrier semaphores. Data moves between devices by JAX's collectives and lax.ppermute only.
A program may use at most 64 MiB of HBM per device.

```python
import math
import jax
import jax.numpy as jnp
from jax import lax

COLS = 8192
B = 256
MOST = 2
CB = 32
NSLAB = 16
BLOCKS = 512
N_FSDP = 64
N_REP = 8


def shared_pattern(key, strength, lower, upper):
    row_part = jax.random.uniform(jax.random.fold_in(key, 21), (NSLAB, B, 1), jnp.float32, lower, upper)
    col_part = jax.random.uniform(jax.random.fold_in(key, 22), (NSLAB, 1, COLS), jnp.float32, lower, upper)
    return strength / N_REP * row_part * col_part


def draw_gradients(key, part):
    key = jax.random.fold_in(key, 9)
    shape = (N_REP, NSLAB, B, COLS)
    noise = 0.02 * jax.random.truncated_normal(jax.random.fold_in(key, 23), -6.0, 6.0, shape, jnp.float32)
    common = shared_pattern(key, 0.15, 0.5, 1.5)
    return (noise + common[None]).astype(jnp.bfloat16)


def draw_owned_blocks(key, part):
    key = jax.random.fold_in(key, 1)
    devices_all = N_FSDP * N_REP
    device_rank = jax.random.permutation(jax.random.fold_in(key, 2), devices_all)
    counts = jnp.where(device_rank < devices_all // 4, 2, jnp.where(device_rank < 3 * devices_all // 4, 1, 0)).astype(jnp.int32)
    starts = jnp.cumsum(counts) - counts
    block_order = jax.random.permutation(jax.random.fold_in(key, 3), BLOCKS).astype(jnp.int32)
    slot_index = jnp.arange(MOST, dtype=jnp.int32)
    position = starts[:, None] + slot_index[None, :]
    is_live = slot_index[None, :] < counts[:, None]
    chosen = jnp.where(is_live, block_order[jnp.minimum(position, BLOCKS - 1)], BLOCKS)
    return chosen.reshape(N_FSDP, N_REP, MOST).astype(jnp.int32)


def root_matrix(key, spread):
    shape = (N_FSDP, N_REP, MOST, B, B)
    noise = jax.random.truncated_normal(jax.random.fold_in(key, 11), -4.0, 4.0, shape, jnp.float32)
    identity = jnp.eye(B, dtype=jnp.float32)
    row_scale = jnp.exp(spread * jax.random.uniform(jax.random.fold_in(key, 12), shape[:-1] + (1,), jnp.float32, -1.0, 1.0))
    return (identity + noise * (0.5 / B ** 0.5)) * row_scale


def draw_left_root(key, part):
    key = jax.random.fold_in(key, 5)
    return root_matrix(key, 0.2).astype(jnp.bfloat16)


def draw_right_root(key, part):
    key = jax.random.fold_in(key, 7)
    return root_matrix(key, 0.2).astype(jnp.bfloat16)


def with_ends(entries, rng, low, high):
    longest = entries.shape.index(max(entries.shape))
    spots = []
    for shift in (0, 1):
        where = [jax.random.randint(jax.random.fold_in(rng, axis), (), 0, length) for axis, length in enumerate(entries.shape)]
        where[longest] = (where[longest] + shift) % entries.shape[longest]
        spots.append(tuple(where))
    return entries.at[spots[0]].set(low).at[spots[1]].set(high)


def block_levels(rng, dims, shards, low, largest):
    level, own = 1.0, jax.random.fold_in(rng, 6)
    for dim, shards_of in shards:
        heights = jnp.exp(jax.random.uniform(jax.random.fold_in(own, dim), (shards_of,), jnp.float32, low / len(shards), largest / len(shards)))
        level = level * jnp.repeat(heights, dims[dim] // shards_of).reshape([-1 if axis == dim else 1 for axis in range(len(dims))])
    return level


def scatter_about(own_key, dims, scale, limit, shards=(), kind=jnp.bfloat16):
    entries = jax.random.normal(own_key, dims, jnp.float32) * scale
    if len(shards) > 0:
        entries = block_levels(own_key, dims, shards, -0.22, 0.18) * entries
    return jnp.clip(entries, min=-limit, max=limit).astype(kind)


def setup_inputs(seed: int = 0) -> dict:
    seeds = jax.random.split(jax.random.key(seed), 10)
    return {
        "gradients": draw_gradients(jax.random.fold_in(seeds[9], 71), 0),
        "owned_blocks": draw_owned_blocks(jax.random.fold_in(seeds[9], 71), 0),
        "rows_valid": with_ends(jax.random.randint(seeds[2], (BLOCKS,), B // 2, B + 1), jax.random.fold_in(seeds[2], 1), B // 2, B).astype(jnp.int32),
        "cols_valid": with_ends(jax.random.randint(seeds[3], (BLOCKS,), B // 2, B + 1), jax.random.fold_in(seeds[3], 1), B // 2, B).astype(jnp.int32),
        "left_factor": scatter_about(seeds[4], (N_FSDP, N_REP, MOST, B, B), 0.5, 3.0, ((0, 64), (1, 8)), jnp.float32),
        "right_factor": scatter_about(seeds[5], (N_FSDP, N_REP, MOST, B, B), 0.5, 3.0, ((0, 64), (1, 8)), jnp.float32),
        "left_root": draw_left_root(jax.random.fold_in(seeds[9], 71), 0),
        "right_root": draw_right_root(jax.random.fold_in(seeds[9], 71), 0),
        "second_moment": jnp.clip(jnp.exp(math.log(0.01) - 4.6051702 * jax.random.uniform(seeds[8], (N_FSDP, N_REP, MOST, B, B), jnp.float32) ** block_levels(seeds[8], (N_FSDP, N_REP, MOST, B, B), ((0, 64), (1, 8)), -0.2, 0.2)), 0.0001, 0.01),
    }


factor_decay = 0.95
moment_decay = 0.999
adam_eps = 1e-08

def reference(gradients, owned_blocks, rows_valid, cols_valid, left_factor, right_factor, left_root, right_root, second_moment):
    summed = lax.optimization_barrier(jnp.sum(gradients.astype(jnp.float32), axis=0)).astype(jnp.bfloat16)
    blocks_all = summed.reshape(NSLAB, B, CB, B).transpose(0, 2, 1, 3).reshape(BLOCKS, B, B)
    slot_ids = owned_blocks.reshape(-1).astype(jnp.int32)
    slots_total = slot_ids.shape[0]
    row_ids = jnp.arange(B, dtype=jnp.int32)

    def per_slot(items):
        block_id, left_old, right_old, left_inv, right_inv, moment_old = items
        present = block_id < BLOCKS
        safe_id = jnp.minimum(block_id, BLOCKS - 1)
        row_limit = jnp.where(present, rows_valid[safe_id], 0)
        col_limit = jnp.where(present, cols_valid[safe_id], 0)
        inside = (row_ids[:, None] < row_limit) & (row_ids[None, :] < col_limit)
        grad_block = jnp.where(inside, blocks_all[safe_id], jnp.zeros((), jnp.bfloat16))
        grad_wide = grad_block.astype(jnp.float32)
        left_next = factor_decay * left_old + (1.0 - factor_decay) * jnp.dot(grad_wide, grad_wide.T, precision=lax.Precision.HIGHEST)
        right_next = factor_decay * right_old + (1.0 - factor_decay) * jnp.dot(grad_wide.T, grad_wide, precision=lax.Precision.HIGHEST)
        halfway = jnp.dot(left_inv, grad_block, preferred_element_type=jnp.float32).astype(jnp.bfloat16)
        precond = jnp.dot(halfway, right_inv, preferred_element_type=jnp.float32)
        precond = jnp.where(inside, precond, jnp.float32(0.0))
        moment = moment_decay * moment_old + (1.0 - moment_decay) * grad_wide * grad_wide
        adam = grad_wide / (jnp.sqrt(moment) + adam_eps)
        adam_norm = jnp.sqrt(jnp.sum(adam * adam))
        pre_norm = jnp.sqrt(jnp.sum(precond * precond) + 1e-06)
        slot_update = (precond * (adam_norm / pre_norm)).astype(jnp.bfloat16)
        return (slot_update, left_next, right_next)
    shaped = (slots_total, B, B)
    outputs = lax.map(per_slot, (slot_ids, left_factor.reshape(shaped), right_factor.reshape(shaped), left_root.reshape(shaped), right_root.reshape(shaped), second_moment.reshape(shaped)))
    slot_update, left_next, right_next = outputs
    placed = jnp.zeros((BLOCKS, B, B), jnp.bfloat16).at[slot_ids].set(slot_update, mode='drop')
    update = placed.reshape(NSLAB, CB, B, B).transpose(0, 2, 1, 3).reshape(NSLAB, B, COLS)
    return (update, left_next.reshape(left_factor.shape), right_next.reshape(right_factor.shape))
```

```python
import jax
import jax.numpy as jnp
from jax import lax
from jax.sharding import PartitionSpec as P

factor_decay = 0.95
moment_decay = 0.999
adam_eps = 1e-08


def body(
    gradients,
    owned_blocks,
    rows_valid,
    cols_valid,
    left_factor,
    right_factor,
    left_root,
    right_root,
    second_moment,
):
    shards = lax.axis_size("fsdp")
    copies = lax.axis_size("rep")
    owners = shards * copies
    shard_index = lax.axis_index("fsdp")
    copy_index = lax.axis_index("rep")
    slab_count, row_count, col_count = gradients.shape[1:]
    size_b = left_factor.shape[-1]
    col_blocks = col_count // size_b
    slot_count = owned_blocks.shape[2]
    block_total = slab_count * col_blocks

    def shifted(operand, by):
        return lax.ppermute(operand, "rep", [(i, (i + by) % copies) for i in range(copies)])

    def crossed(operand, by):
        pairs = []
        for owner in range(shards):
            step = by if owner % 2 == 0 else -by
            pairs += [
                (owner * copies + i, owner * copies + (i + step) % copies) for i in range(copies)
            ]
        return lax.ppermute(operand, ("fsdp", "rep"), pairs)

    rows = (
        gradients[0]
        .reshape(slab_count, row_count, col_blocks, size_b)
        .transpose(1, 0, 2, 3)
        .reshape(row_count, block_total, size_b)
    )

    def row_at(by):
        return lax.dynamic_index_in_dim(rows, (copy_index + by) % row_count, 0, keepdims=False)

    from_two = crossed(row_at(2), 2)
    from_left = shifted(row_at(1), 1)
    from_right = shifted(row_at(3), -1)
    summed = lax.optimization_barrier(
        (
            row_at(0).astype(jnp.float32)
            + from_left.astype(jnp.float32)
            + from_right.astype(jnp.float32)
            + from_two.astype(jnp.float32)
        ).astype(jnp.bfloat16)
    )
    slot_ids = owned_blocks.reshape(-1)
    block_ids = jnp.arange(block_total, dtype=jnp.int32)
    pick = (slot_ids[:, None] == block_ids[None, :]).astype(jnp.bfloat16)
    outgoing = (
        jnp.dot(pick, summed, preferred_element_type=jnp.float32)
        .astype(jnp.bfloat16)
        .reshape(owners, slot_count, size_b)
    )
    mine = lax.all_to_all(outgoing, ("fsdp", "rep"), split_axis=0, concat_axis=0, tiled=True)
    blocks = (
        mine.reshape(shards, copies // row_count, row_count, slot_count, size_b)
        .astype(jnp.float32)
        .sum(axis=1)
        .transpose(2, 0, 1, 3)
        .reshape(slot_count, size_b, size_b)
        .astype(jnp.bfloat16)
    )
    owned_here = owned_blocks[shard_index, copy_index]
    row_limit = jnp.take(rows_valid, owned_here, mode="fill", fill_value=0)
    col_limit = jnp.take(cols_valid, owned_here, mode="fill", fill_value=0)
    row_ids = jnp.arange(size_b, dtype=jnp.int32)
    inside = (row_ids[None, :, None] < row_limit[:, None, None]) & (
        row_ids[None, None, :] < col_limit[:, None, None]
    )
    grad_block = jnp.where(inside, blocks, jnp.zeros((), jnp.bfloat16))
    grad_wide = grad_block.astype(jnp.float32)
    left_next = factor_decay * left_factor[0, 0] + (1.0 - factor_decay) * jnp.einsum(
        "kij,klj->kil", grad_block, grad_block, preferred_element_type=jnp.float32
    )
    right_next = factor_decay * right_factor[0, 0] + (1.0 - factor_decay) * jnp.einsum(
        "kji,kjl->kil", grad_block, grad_block, preferred_element_type=jnp.float32
    )
    halfway = jnp.einsum(
        "kij,kjl->kil", left_root[0, 0], grad_block, preferred_element_type=jnp.float32
    ).astype(jnp.bfloat16)
    precond = jnp.einsum(
        "kij,kjl->kil", halfway, right_root[0, 0], preferred_element_type=jnp.float32
    )
    precond = jnp.where(inside, precond, jnp.float32(0.0))
    moment = moment_decay * second_moment[0, 0] + (1.0 - moment_decay) * grad_wide * grad_wide
    adam = grad_wide / (jnp.sqrt(moment) + adam_eps)
    adam_norm = jnp.sqrt(jnp.sum(adam * adam, axis=(1, 2)))
    pre_norm = jnp.sqrt(jnp.sum(precond * precond, axis=(1, 2)) + 1e-06)
    slot_update = (precond * (adam_norm / pre_norm)[:, None, None]).astype(jnp.bfloat16)
    by_row = slot_update.reshape(slot_count, shards, 1, row_count, size_b).transpose(1, 2, 3, 0, 4)
    parts_out = jnp.broadcast_to(
        by_row, (shards, copies // row_count, row_count, slot_count, size_b)
    ).reshape(owners, slot_count, size_b)
    returned = lax.all_to_all(parts_out, ("fsdp", "rep"), split_axis=0, concat_axis=0, tiled=True)
    place = (block_ids[:, None] == slot_ids[None, :]).astype(jnp.bfloat16)
    placed = jnp.dot(
        place, returned.reshape(owners * slot_count, size_b), preferred_element_type=jnp.float32
    ).astype(jnp.bfloat16)
    row_two = crossed(placed, 2)
    row_one = shifted(placed, -1)
    row_three = shifted(placed, 1)
    gathered = jnp.zeros((row_count, block_total, size_b), jnp.bfloat16)
    for by, entries in enumerate((placed, row_one, row_two, row_three)):
        gathered = lax.dynamic_update_index_in_dim(
            gathered, entries, (copy_index + by) % row_count, 0
        )
    update = (
        gathered.reshape(row_count, slab_count, col_blocks, size_b)
        .transpose(1, 0, 2, 3)
        .reshape(slab_count, row_count, col_count)
    )
    return (update, left_next[None, None], right_next[None, None])


def solution(mesh):
    in_specs = (
        P("rep", None, "fsdp", None),
        P(),
        P(),
        P(),
        P("fsdp", "rep", None, None, None),
        P("fsdp", "rep", None, None, None),
        P("fsdp", "rep", None, None, None),
        P("fsdp", "rep", None, None, None),
        P("fsdp", "rep", None, None, None),
    )
    out_specs = (
        P(None, "fsdp", None),
        P("fsdp", "rep", None, None, None),
        P("fsdp", "rep", None, None, None),
    )
    return jax.shard_map(body, mesh=mesh, in_specs=in_specs, out_specs=out_specs, check_vma=False)
```

```python
import functools

import jax
import jax.numpy as jnp
from jax import lax
from jax.experimental import pallas as pl
from jax.experimental.pallas import tpu as pltpu
from jax.sharding import PartitionSpec as P

factor_decay = 0.95
moment_decay = 0.999
adam_eps = 1e-08
LANES = 128
BF16 = jnp.bfloat16
F32 = jnp.float32


def call(kernel, out_shape, scratch_shapes, in_spaces, out_space=pltpu.VMEM, limit=32 * 1024 * 1024):
    return pl.pallas_call(
        kernel,
        out_shape=out_shape,
        in_specs=[pl.BlockSpec(memory_space=space) for space in in_spaces],
        out_specs=jax.tree.map(lambda _: pl.BlockSpec(memory_space=out_space), out_shape),
        scratch_shapes=list(scratch_shapes),
        compiler_params=pltpu.CompilerParams(vmem_limit_bytes=limit),
    )


def row_order(row_count):
    here = lax.axis_index("rep")
    turn = 2 * lax.rem(lax.axis_index("fsdp"), 2)
    return [lax.rem(here + by, row_count) for by in (0, 2, 1 + turn, 3 - turn)]


def split_kernel(row_count, halves, chosen, grads_ref, *refs):
    rows_at = row_order(row_count)
    outs, wide = refs[:-1], refs[-1]
    step = row_count * halves
    wide[...] = grads_ref[...].astype(F32)
    for n, out in zip(chosen, outs):
        for half in range(halves):
            part = wide[pl.ds(half * row_count + rows_at[n], out.shape[0], stride=step), :]
            out[:, half * LANES : (half + 1) * LANES] = part.astype(BF16)


def join_kernel(row_count, halves, *refs):
    rows_at = row_order(row_count)
    ins, (out_ref, near, wide, sems) = refs[:row_count], refs[row_count:]
    step = row_count * halves
    chunks = sems.shape[0]
    size = near.shape[0] // chunks
    copies = []
    for chunk in range(chunks):
        first, last = chunk * size, (chunk + 1) * size
        for n, rows in enumerate(ins):
            for half in range(halves):
                start = first + half * row_count + rows_at[n]
                part = rows[first // step : last // step, half * LANES : (half + 1) * LANES]
                wide[pl.ds(start, size // step, stride=step), :] = part.astype(F32)
        near[first:last, :] = wide[first:last, :].astype(BF16)
        span = pl.ds(first, size)
        copy = pltpu.make_async_copy(near.at[span], out_ref.at[span], sems.at[chunk])
        copy.start()
        copies.append(copy)
    for copy in copies:
        copy.wait()


def pick_kernel(halves, pick_ref, own_ref, two_ref, one_ref, three_ref, out_ref, wide):
    slots, owners = pick_ref.shape[:2]
    total = (
        own_ref[...].astype(F32)
        + one_ref[...].astype(F32)
        + two_ref[...].astype(F32)
        + three_ref[...].astype(F32)
    ).astype(BF16)
    for slot in range(slots):
        rows = jnp.dot(pick_ref[slot], total, preferred_element_type=F32)
        for half in range(halves):
            wide[pl.ds(half * slots + slot, owners, stride=halves * slots), :] = rows[
                :, half * LANES : (half + 1) * LANES
            ]
    out_ref[...] = wide[...].astype(BF16)


def place_kernel(halves, place_ref, got_ref, out_ref, wide):
    slots, _, owners = place_ref.shape
    wide[...] = got_ref[...].astype(F32)
    for half in range(halves):
        rows = 0.0
        for slot in range(slots):
            part = wide[pl.ds(half * slots + slot, owners, stride=halves * slots), :].astype(BF16)
            rows = rows + jnp.dot(place_ref[slot], part, preferred_element_type=F32)
        out_ref[:, half * LANES : (half + 1) * LANES] = rows.astype(BF16)


def update_kernel(
    halves, limits_ref, gather_ref, got_ref, lroot_ref, rroot_ref, moment_ref,
    grad_ref, out_ref, wide, wide_out,
):
    slots, size = grad_ref.shape[:2]
    owners = gather_ref.shape[1]
    step = slots * halves
    wide[...] = got_ref[...].astype(F32)
    row_ids = lax.broadcasted_iota(jnp.int32, (size, size), 0)
    col_ids = lax.broadcasted_iota(jnp.int32, (size, size), 1)
    for slot in range(slots):
        inside = (row_ids < limits_ref[0, slot]) & (col_ids < limits_ref[1, slot])
        parts = [
            wide[pl.ds(half * slots + slot, owners, stride=step), :].astype(BF16)
            for half in range(halves)
        ]
        block = jnp.dot(
            gather_ref[...], jnp.concatenate(parts, axis=1), preferred_element_type=F32
        ).astype(BF16)
        grad_wide = jnp.where(inside, block.astype(F32), 0.0)
        grad = grad_wide.astype(BF16)
        grad_ref[slot] = grad
        halfway = jnp.dot(lroot_ref[slot], grad, preferred_element_type=F32).astype(BF16)
        precond = jnp.dot(halfway, rroot_ref[slot], preferred_element_type=F32)
        precond = jnp.where(inside, precond, 0.0)
        moment = moment_decay * moment_ref[slot] + (1.0 - moment_decay) * grad_wide * grad_wide
        adam = grad_wide / (jnp.sqrt(moment) + adam_eps)
        adam_norm = jnp.sqrt(jnp.sum(adam * adam, axis=(0, 1), keepdims=True))
        pre_norm = jnp.sqrt(jnp.sum(precond * precond, axis=(0, 1), keepdims=True) + 1e-06)
        slot_update = (precond * (adam_norm / pre_norm)).astype(BF16)
        rows = lax.dot_general(
            gather_ref[...], slot_update, (((0,), (0,)), ((), ())), preferred_element_type=F32
        )
        for half in range(halves):
            wide_out[pl.ds(half * slots + slot, owners, stride=step), :] = rows[
                :, half * LANES : (half + 1) * LANES
            ]
    out_ref[...] = wide_out[...].astype(BF16)


def body(
    gradients,
    owned_blocks,
    rows_valid,
    cols_valid,
    left_factor,
    right_factor,
    left_root,
    right_root,
    second_moment,
):
    shards = lax.axis_size("fsdp")
    copies = lax.axis_size("rep")
    owners = shards * copies
    shard_index = lax.axis_index("fsdp")
    copy_index = lax.axis_index("rep")
    slab_count, row_count, col_count = gradients.shape[1:]
    size_b = left_factor.shape[-1]
    slot_count = owned_blocks.shape[2]
    block_total = slab_count * (col_count // size_b)
    halves = size_b // LANES
    tiles = col_count // LANES
    def crossed(operand, by):
        pairs = []
        for owner in range(shards):
            step = by if owner % 2 == 0 else -by
            pairs += [
                (owner * copies + i, owner * copies + (i + step) % copies) for i in range(copies)
            ]
        return lax.ppermute(operand, ("fsdp", "rep"), pairs)

    def everywhere(operand):
        return lax.all_to_all(operand, ("fsdp", "rep"), split_axis=0, concat_axis=0, tiled=True)

    rows_shape = jax.ShapeDtypeStruct((block_total, size_b), BF16)
    sent_shape = jax.ShapeDtypeStruct((owners * halves * slot_count, LANES), BF16)
    tile_rows = slab_count * tiles * row_count
    near_grads = pltpu.VMEM((tile_rows, LANES), BF16)
    wide_grads = pltpu.VMEM((tile_rows, LANES), F32)
    chunk_sems = pltpu.SemaphoreType.DMA((4,))
    wide_sent = pltpu.VMEM(sent_shape.shape, F32)

    by_tile = (
        gradients[0]
        .reshape(slab_count, row_count, tiles, LANES)
        .transpose(0, 2, 1, 3)
        .reshape(tile_rows, LANES)
    )
    (row_two,) = call(
        functools.partial(split_kernel, row_count, halves, (1,)),
        (rows_shape,),
        [wide_grads],
        [pltpu.VMEM],
    )(by_tile)
    by_tile, row_two = lax.optimization_barrier((by_tile, row_two))
    from_two = crossed(row_two, 2)
    row_zero, row_one, row_three = call(
        functools.partial(split_kernel, row_count, halves, (0, 2, 3)),
        (rows_shape,) * 3,
        [wide_grads],
        [pltpu.VMEM],
    )(by_tile)
    from_one = crossed(row_one, 1)
    from_three = crossed(row_three, -1)
    slot_ids = owned_blocks.reshape(owners, slot_count).T
    block_ids = jnp.arange(block_total, dtype=jnp.int32)
    pick = (slot_ids[:, :, None] == block_ids[None, None, :]).astype(BF16)
    place = (slot_ids[:, None, :] == block_ids[None, :, None]).astype(BF16)
    row = jnp.arange(size_b, dtype=jnp.int32)[:, None]
    source = jnp.arange(owners, dtype=jnp.int32)[None, :]
    gather = (
        (row // row_count == source // copies) & (row % row_count == source % row_count)
    ).astype(BF16)
    outgoing = call(
        functools.partial(pick_kernel, halves), sent_shape, [wide_sent], [pltpu.VMEM] * 5
    )(pick, row_zero, from_two, from_one, from_three)
    arrived = everywhere(outgoing)
    owned_here = owned_blocks[shard_index, copy_index]
    row_limit = jnp.take(rows_valid, owned_here, mode="fill", fill_value=0)
    col_limit = jnp.take(cols_valid, owned_here, mode="fill", fill_value=0)
    grad_block, parts_out = call(
        functools.partial(update_kernel, halves),
        (jax.ShapeDtypeStruct((slot_count, size_b, size_b), BF16), sent_shape),
        [wide_sent, wide_sent],
        [pltpu.SMEM] + [pltpu.VMEM] * 5,
    )(
        jnp.stack([row_limit, col_limit]),
        gather,
        arrived,
        left_root[0, 0],
        right_root[0, 0],
        second_moment[0, 0],
    )
    left_next = factor_decay * left_factor[0, 0] + (1.0 - factor_decay) * jnp.einsum(
        "kij,klj->kil", grad_block, grad_block, preferred_element_type=F32
    )
    right_next = factor_decay * right_factor[0, 0] + (1.0 - factor_decay) * jnp.einsum(
        "kji,kjl->kil", grad_block, grad_block, preferred_element_type=F32
    )
    returned = everywhere(parts_out)
    returned, left_next, right_next = lax.optimization_barrier((returned, left_next, right_next))
    placed = call(
        functools.partial(place_kernel, halves), rows_shape, [wide_sent], [pltpu.VMEM] * 2
    )(place, returned)
    row_two = crossed(placed, 2)
    row_one = crossed(placed, 1)
    row_three = crossed(placed, -1)
    joined = call(
        functools.partial(join_kernel, row_count, halves),
        jax.ShapeDtypeStruct((tile_rows, LANES), BF16),
        [near_grads, wide_grads, chunk_sems],
        [pltpu.VMEM] * row_count,
        out_space=pltpu.HBM,
    )(placed, row_two, row_three, row_one)
    update = (
        joined.reshape(slab_count, tiles, row_count, LANES)
        .transpose(0, 2, 1, 3)
        .reshape(slab_count, row_count, col_count)
    )
    return (update, left_next[None, None], right_next[None, None])


def solution(mesh):
    in_specs = (
        P("rep", None, "fsdp", None),
        P(),
        P(),
        P(),
        P("fsdp", "rep", None, None, None),
        P("fsdp", "rep", None, None, None),
        P("fsdp", "rep", None, None, None),
        P("fsdp", "rep", None, None, None),
        P("fsdp", "rep", None, None, None),
    )
    out_specs = (
        P(None, "fsdp", None),
        P("fsdp", "rep", None, None, None),
        P("fsdp", "rep", None, None, None),
    )
    return jax.shard_map(body, mesh=mesh, in_specs=in_specs, out_specs=out_specs, check_vma=False)
```

```python
import functools

import jax
import jax.numpy as jnp
from jax import lax
from jax.experimental import pallas as pl
from jax.experimental.pallas import tpu as pltpu
from jax.sharding import PartitionSpec as P

factor_decay = 0.95
moment_decay = 0.999
adam_eps = 1e-08
LANES = 128
BF16 = jnp.bfloat16
F32 = jnp.float32


def call(kernel, out_shape, scratch_shapes, in_spaces, out_space=pltpu.VMEM, limit=32 * 1024 * 1024):
    return pl.pallas_call(
        kernel,
        out_shape=out_shape,
        in_specs=[pl.BlockSpec(memory_space=space) for space in in_spaces],
        out_specs=jax.tree.map(lambda _: pl.BlockSpec(memory_space=out_space), out_shape),
        scratch_shapes=list(scratch_shapes),
        compiler_params=pltpu.CompilerParams(vmem_limit_bytes=limit),
    )


def row_order(row_count):
    here = lax.axis_index("rep")
    turn = 2 * lax.rem(lax.axis_index("fsdp"), 2)
    return [lax.rem(here + by, row_count) for by in (0, 2, 1 + turn, 3 - turn)]


def split_kernel(row_count, halves, grads_ref, *refs):
    rows_at = row_order(row_count)
    outs, wide = refs[:-1], refs[-1]
    step = row_count * halves
    wide[...] = grads_ref[...].astype(F32)
    for n, out in enumerate(outs):
        for half in range(halves):
            part = wide[pl.ds(half * row_count + rows_at[n], out.shape[0], stride=step), :]
            out[:, half * LANES : (half + 1) * LANES] = part.astype(BF16)


def join_kernel(row_count, halves, *refs):
    rows_at = row_order(row_count)
    ins, (out_ref, near, wide, sems) = refs[:row_count], refs[row_count:]
    step = row_count * halves
    chunks = sems.shape[0]
    size = near.shape[0] // chunks
    copies = []
    for chunk in range(chunks):
        first, last = chunk * size, (chunk + 1) * size
        for n, rows in enumerate(ins):
            for half in range(halves):
                start = first + half * row_count + rows_at[n]
                part = rows[first // step : last // step, half * LANES : (half + 1) * LANES]
                wide[pl.ds(start, size // step, stride=step), :] = part.astype(F32)
        near[first:last, :] = wide[first:last, :].astype(BF16)
        span = pl.ds(first, size)
        copy = pltpu.make_async_copy(near.at[span], out_ref.at[span], sems.at[chunk])
        copy.start()
        copies.append(copy)
    for copy in copies:
        copy.wait()


def pick_kernel(halves, pick_ref, own_ref, two_ref, one_ref, three_ref, out_ref, wide):
    slots, owners = pick_ref.shape[:2]
    total = (
        own_ref[...].astype(F32)
        + one_ref[...].astype(F32)
        + two_ref[...].astype(F32)
        + three_ref[...].astype(F32)
    ).astype(BF16)
    for slot in range(slots):
        rows = jnp.dot(pick_ref[slot], total, preferred_element_type=F32)
        for half in range(halves):
            wide[pl.ds(half * slots + slot, owners, stride=halves * slots), :] = rows[
                :, half * LANES : (half + 1) * LANES
            ]
    out_ref[...] = wide[...].astype(BF16)


def place_kernel(halves, place_ref, got_ref, out_ref, wide):
    slots, _, owners = place_ref.shape
    wide[...] = got_ref[...].astype(F32)
    rows = 0.0
    for slot in range(slots):
        parts = [
            wide[pl.ds(half * slots + slot, owners, stride=halves * slots), :].astype(BF16)
            for half in range(halves)
        ]
        rows = rows + jnp.dot(
            place_ref[slot], jnp.concatenate(parts, axis=1), preferred_element_type=F32
        )
    out_ref[...] = rows.astype(BF16)


def update_kernel(
    halves, limits_ref, gather_ref, got_ref, lroot_ref, rroot_ref, moment_ref,
    grad_ref, out_ref, wide, wide_out,
):
    slots, size = grad_ref.shape[:2]
    owners = gather_ref.shape[1]
    step = slots * halves
    every = range(slots)
    wide[...] = got_ref[...].astype(F32)
    row_ids = lax.broadcasted_iota(jnp.int32, (size, size), 0)
    col_ids = lax.broadcasted_iota(jnp.int32, (size, size), 1)
    parts = [
        wide[pl.ds(half * slots + slot, owners, stride=step), :].astype(BF16)
        for slot in every
        for half in range(halves)
    ]
    blocks = jnp.dot(
        gather_ref[...], jnp.concatenate(parts, axis=1), preferred_element_type=F32
    ).astype(BF16)
    inside, wides, grads = [], [], []
    for slot in every:
        inside.append((row_ids < limits_ref[0, slot]) & (col_ids < limits_ref[1, slot]))
        block = blocks[:, slot * size : (slot + 1) * size].astype(F32)
        wides.append(jnp.where(inside[slot], block, 0.0))
        grads.append(wides[slot].astype(BF16))
        grad_ref[slot] = grads[slot]
    halfway = [
        jnp.dot(lroot_ref[slot], grads[slot], preferred_element_type=F32).astype(BF16)
        for slot in every
    ]
    preconds = [
        jnp.where(
            inside[slot], jnp.dot(halfway[slot], rroot_ref[slot], preferred_element_type=F32), 0.0
        )
        for slot in every
    ]
    updates = []
    for slot, (grad_wide, precond) in enumerate(zip(wides, preconds)):
        moment = moment_decay * moment_ref[slot] + (1.0 - moment_decay) * grad_wide * grad_wide
        adam = grad_wide / (jnp.sqrt(moment) + adam_eps)
        adam_norm = jnp.sqrt(jnp.sum(adam * adam, axis=(0, 1), keepdims=True))
        pre_norm = jnp.sqrt(jnp.sum(precond * precond, axis=(0, 1), keepdims=True) + 1e-06)
        updates.append((precond * (adam_norm / pre_norm)).astype(BF16))
    rows = lax.dot_general(
        gather_ref[...],
        jnp.concatenate(updates, axis=1),
        (((0,), (0,)), ((), ())),
        preferred_element_type=F32,
    )
    for slot in every:
        for half in range(halves):
            first = slot * size + half * LANES
            wide_out[pl.ds(half * slots + slot, owners, stride=step), :] = rows[
                :, first : first + LANES
            ]
    out_ref[...] = wide_out[...].astype(BF16)


def body(
    gradients,
    owned_blocks,
    rows_valid,
    cols_valid,
    left_factor,
    right_factor,
    left_root,
    right_root,
    second_moment,
):
    shards = lax.axis_size("fsdp")
    copies = lax.axis_size("rep")
    owners = shards * copies
    shard_index = lax.axis_index("fsdp")
    copy_index = lax.axis_index("rep")
    slab_count, row_count, col_count = gradients.shape[1:]
    size_b = left_factor.shape[-1]
    slot_count = owned_blocks.shape[2]
    block_total = slab_count * (col_count // size_b)
    halves = size_b // LANES
    tiles = col_count // LANES
    def crossed(operand, by):
        pairs = []
        for owner in range(shards):
            step = by if owner % 2 == 0 else -by
            pairs += [
                (owner * copies + i, owner * copies + (i + step) % copies) for i in range(copies)
            ]
        return lax.ppermute(operand, ("fsdp", "rep"), pairs)

    def everywhere(operand):
        return lax.all_to_all(operand, ("fsdp", "rep"), split_axis=0, concat_axis=0, tiled=True)

    rows_shape = jax.ShapeDtypeStruct((block_total, size_b), BF16)
    sent_shape = jax.ShapeDtypeStruct((owners * halves * slot_count, LANES), BF16)
    tile_rows = slab_count * tiles * row_count
    near_grads = pltpu.VMEM((tile_rows, LANES), BF16)
    wide_grads = pltpu.VMEM((tile_rows, LANES), F32)
    chunk_sems = pltpu.SemaphoreType.DMA((4,))
    wide_sent = pltpu.VMEM(sent_shape.shape, F32)

    by_tile = (
        gradients[0]
        .reshape(slab_count, row_count, tiles, LANES)
        .transpose(0, 2, 1, 3)
        .reshape(tile_rows, LANES)
    )
    row_zero, row_two, row_one, row_three = call(
        functools.partial(split_kernel, row_count, halves),
        (rows_shape,) * row_count,
        [wide_grads],
        [pltpu.VMEM],
    )(by_tile)
    from_two = crossed(row_two, 2)
    from_one = crossed(row_one, 1)
    from_three = crossed(row_three, -1)
    slot_ids = owned_blocks.reshape(owners, slot_count).T
    block_ids = jnp.arange(block_total, dtype=jnp.int32)
    pick = (slot_ids[:, :, None] == block_ids[None, None, :]).astype(BF16)
    place = (slot_ids[:, None, :] == block_ids[None, :, None]).astype(BF16)
    row = jnp.arange(size_b, dtype=jnp.int32)[:, None]
    source = jnp.arange(owners, dtype=jnp.int32)[None, :]
    gather = (
        (row // row_count == source // copies) & (row % row_count == source % row_count)
    ).astype(BF16)
    outgoing = call(
        functools.partial(pick_kernel, halves), sent_shape, [wide_sent], [pltpu.VMEM] * 5
    )(pick, row_zero, from_two, from_one, from_three)
    owned_here = owned_blocks[shard_index, copy_index]
    row_limit = jnp.take(rows_valid, owned_here, mode="fill", fill_value=0)
    col_limit = jnp.take(cols_valid, owned_here, mode="fill", fill_value=0)
    limits = jnp.stack([row_limit, col_limit])
    outgoing, limits, gather = lax.optimization_barrier((outgoing, limits, gather))
    arrived = everywhere(outgoing)
    grad_block, parts_out = call(
        functools.partial(update_kernel, halves),
        (jax.ShapeDtypeStruct((slot_count, size_b, size_b), BF16), sent_shape),
        [wide_sent, wide_sent],
        [pltpu.SMEM] + [pltpu.VMEM] * 5,
    )(
        limits,
        gather,
        arrived,
        left_root[0, 0],
        right_root[0, 0],
        second_moment[0, 0],
    )
    returned = everywhere(parts_out)
    placed = call(
        functools.partial(place_kernel, halves), rows_shape, [wide_sent], [pltpu.VMEM] * 2
    )(place, returned)
    row_two = crossed(placed, 2)
    row_one = crossed(placed, 1)
    row_three = crossed(placed, -1)
    row_two, grad_block = lax.optimization_barrier((row_two, grad_block))
    left_next = factor_decay * left_factor[0, 0] + (1.0 - factor_decay) * jnp.einsum(
        "kij,klj->kil", grad_block, grad_block, preferred_element_type=F32
    )
    right_next = factor_decay * right_factor[0, 0] + (1.0 - factor_decay) * jnp.einsum(
        "kji,kjl->kil", grad_block, grad_block, preferred_element_type=F32
    )
    joined = call(
        functools.partial(join_kernel, row_count, halves),
        jax.ShapeDtypeStruct((tile_rows, LANES), BF16),
        [near_grads, wide_grads, chunk_sems],
        [pltpu.VMEM] * row_count,
        out_space=pltpu.HBM,
    )(placed, row_two, row_three, row_one)
    update = (
        joined.reshape(slab_count, tiles, row_count, LANES)
        .transpose(0, 2, 1, 3)
        .reshape(slab_count, row_count, col_count)
    )
    return (update, left_next[None, None], right_next[None, None])


def solution(mesh):
    in_specs = (
        P("rep", None, "fsdp", None),
        P(),
        P(),
        P(),
        P("fsdp", "rep", None, None, None),
        P("fsdp", "rep", None, None, None),
        P("fsdp", "rep", None, None, None),
        P("fsdp", "rep", None, None, None),
        P("fsdp", "rep", None, None, None),
    )
    out_specs = (
        P(None, "fsdp", None),
        P("fsdp", "rep", None, None, None),
        P("fsdp", "rep", None, None, None),
    )
    return jax.shard_map(body, mesh=mesh, in_specs=in_specs, out_specs=out_specs, check_vma=False)
```

```python
import functools

import jax
import jax.numpy as jnp
from jax import lax
from jax.experimental import pallas as pl
from jax.experimental.pallas import tpu as pltpu
from jax.sharding import PartitionSpec as P

factor_decay = 0.95
moment_decay = 0.999
adam_eps = 1e-08
LANES = 128
BF16 = jnp.bfloat16
F32 = jnp.float32


def call(kernel, out_shape, scratch_shapes, in_spaces, out_space=pltpu.VMEM, limit=32 * 1024 * 1024):
    return pl.pallas_call(
        kernel,
        out_shape=out_shape,
        in_specs=[pl.BlockSpec(memory_space=space) for space in in_spaces],
        out_specs=jax.tree.map(lambda _: pl.BlockSpec(memory_space=out_space), out_shape),
        scratch_shapes=list(scratch_shapes),
        compiler_params=pltpu.CompilerParams(vmem_limit_bytes=limit),
    )


def row_order(row_count):
    here = lax.axis_index("rep")
    turn = 2 * lax.rem(lax.axis_index("fsdp"), 2)
    return [lax.rem(here + by, row_count) for by in (0, 2, 1 + turn, 3 - turn)]


def split_kernel(row_count, halves, grads_ref, *refs):
    rows_at = row_order(row_count)
    outs, (near, wide, sems) = refs[:-3], refs[-3:]
    step = row_count * halves
    chunks = sems.shape[0]
    size = near.shape[0] // chunks
    copies = []
    for chunk in range(chunks):
        span = pl.ds(chunk * size, size)
        copy = pltpu.make_async_copy(grads_ref.at[span], near.at[span], sems.at[chunk])
        copy.start()
        copies.append(copy)
    for chunk, copy in enumerate(copies):
        copy.wait()
        first, last = chunk * size, (chunk + 1) * size
        wide[first:last, :] = near[first:last, :].astype(F32)
        for n, out in enumerate(outs):
            for half in range(halves):
                start = first + half * row_count + rows_at[n]
                part = wide[pl.ds(start, size // step, stride=step), :]
                out[first // step : last // step, half * LANES : (half + 1) * LANES] = part.astype(
                    BF16
                )


def join_kernel(row_count, halves, *refs):
    rows_at = row_order(row_count)
    ins, (out_ref, near, wide, sems) = refs[:row_count], refs[row_count:]
    step = row_count * halves
    chunks = sems.shape[0]
    size = near.shape[0] // chunks
    copies = []
    for chunk in range(chunks):
        first, last = chunk * size, (chunk + 1) * size
        for n, rows in enumerate(ins):
            for half in range(halves):
                start = first + half * row_count + rows_at[n]
                part = rows[first // step : last // step, half * LANES : (half + 1) * LANES]
                wide[pl.ds(start, size // step, stride=step), :] = part.astype(F32)
        near[first:last, :] = wide[first:last, :].astype(BF16)
        span = pl.ds(first, size)
        copy = pltpu.make_async_copy(near.at[span], out_ref.at[span], sems.at[chunk])
        copy.start()
        copies.append(copy)
    for copy in copies:
        copy.wait()


def pick_kernel(halves, pick_ref, own_ref, two_ref, one_ref, three_ref, out_ref, wide):
    slots, owners = pick_ref.shape[:2]
    total = (
        own_ref[...].astype(F32)
        + one_ref[...].astype(F32)
        + two_ref[...].astype(F32)
        + three_ref[...].astype(F32)
    ).astype(BF16)
    for slot in range(slots):
        rows = jnp.dot(pick_ref[slot], total, preferred_element_type=F32)
        for half in range(halves):
            wide[pl.ds(half * slots + slot, owners, stride=halves * slots), :] = rows[
                :, half * LANES : (half + 1) * LANES
            ]
    out_ref[...] = wide[: out_ref.shape[0], :].astype(BF16)


def place_kernel(halves, place_ref, got_ref, out_ref, wide):
    slots, _, owners = place_ref.shape
    wide[: got_ref.shape[0], :] = got_ref[...].astype(F32)
    rows = 0.0
    for slot in range(slots):
        parts = [
            wide[pl.ds(half * slots + slot, owners, stride=halves * slots), :].astype(BF16)
            for half in range(halves)
        ]
        rows = rows + jnp.dot(
            place_ref[slot], jnp.concatenate(parts, axis=1), preferred_element_type=F32
        )
    out_ref[...] = rows.astype(BF16)


def update_kernel(
    halves, limits_ref, gather_ref, got_ref, lroot_ref, rroot_ref, moment_ref,
    grad_ref, out_ref, wide, wide_out,
):
    slots, size = grad_ref.shape[:2]
    owners = gather_ref.shape[1]
    step = slots * halves
    every = range(slots)
    wide[: got_ref.shape[0], :] = got_ref[...].astype(F32)
    row_ids = lax.broadcasted_iota(jnp.int32, (size, size), 0)
    col_ids = lax.broadcasted_iota(jnp.int32, (size, size), 1)
    parts = [
        wide[pl.ds(half * slots + slot, owners, stride=step), :].astype(BF16)
        for slot in every
        for half in range(halves)
    ]
    blocks = jnp.dot(
        gather_ref[...], jnp.concatenate(parts, axis=1), preferred_element_type=F32
    ).astype(BF16)
    inside, wides, grads = [], [], []
    for slot in every:
        inside.append((row_ids < limits_ref[0, slot]) & (col_ids < limits_ref[1, slot]))
        block = blocks[:, slot * size : (slot + 1) * size].astype(F32)
        wides.append(jnp.where(inside[slot], block, 0.0))
        grads.append(wides[slot].astype(BF16))
        grad_ref[slot] = grads[slot]
    halfway = [
        jnp.dot(lroot_ref[slot], grads[slot], preferred_element_type=F32).astype(BF16)
        for slot in every
    ]
    preconds = [
        jnp.where(
            inside[slot], jnp.dot(halfway[slot], rroot_ref[slot], preferred_element_type=F32), 0.0
        )
        for slot in every
    ]
    updates = []
    for slot, (grad_wide, precond) in enumerate(zip(wides, preconds)):
        moment = moment_decay * moment_ref[slot] + (1.0 - moment_decay) * grad_wide * grad_wide
        adam = grad_wide / (jnp.sqrt(moment) + adam_eps)
        adam_norm = jnp.sqrt(jnp.sum(adam * adam, axis=(0, 1), keepdims=True))
        pre_norm = jnp.sqrt(jnp.sum(precond * precond, axis=(0, 1), keepdims=True) + 1e-06)
        updates.append((precond * (adam_norm / pre_norm)).astype(BF16))
    rows = lax.dot_general(
        gather_ref[...],
        jnp.concatenate(updates, axis=1),
        (((0,), (0,)), ((), ())),
        preferred_element_type=F32,
    )
    for slot in every:
        for half in range(halves):
            first = slot * size + half * LANES
            wide_out[pl.ds(half * slots + slot, owners, stride=step), :] = rows[
                :, first : first + LANES
            ]
    out_ref[...] = wide_out[: out_ref.shape[0], :].astype(BF16)


def body(
    gradients,
    owned_blocks,
    rows_valid,
    cols_valid,
    left_factor,
    right_factor,
    left_root,
    right_root,
    second_moment,
):
    shards = lax.axis_size("fsdp")
    copies = lax.axis_size("rep")
    owners = shards * copies
    shard_index = lax.axis_index("fsdp")
    copy_index = lax.axis_index("rep")
    slab_count, row_count, col_count = gradients.shape[1:]
    size_b = left_factor.shape[-1]
    slot_count = owned_blocks.shape[2]
    block_total = slab_count * (col_count // size_b)
    halves = size_b // LANES
    tiles = col_count // LANES
    def crossed(operand, by):
        pairs = []
        for owner in range(shards):
            step = by if owner % 2 == 0 else -by
            pairs += [
                (owner * copies + i, owner * copies + (i + step) % copies) for i in range(copies)
            ]
        return lax.ppermute(operand, ("fsdp", "rep"), pairs)

    def everywhere(operand):
        return lax.all_to_all(operand, ("fsdp", "rep"), split_axis=0, concat_axis=0, tiled=True)

    rows_shape = jax.ShapeDtypeStruct((block_total, size_b), BF16)
    sent_shape = jax.ShapeDtypeStruct((owners * halves * slot_count, LANES), BF16)
    tile_rows = slab_count * tiles * row_count
    near_grads = pltpu.VMEM((tile_rows, LANES), BF16)
    wide_grads = pltpu.VMEM((tile_rows + row_count * halves, LANES), F32)
    chunk_sems = pltpu.SemaphoreType.DMA((4,))
    wide_sent = pltpu.VMEM((sent_shape.shape[0] + 8, LANES), F32)

    by_tile = (
        gradients[0]
        .reshape(slab_count, row_count, tiles, LANES)
        .transpose(0, 2, 1, 3)
        .reshape(tile_rows, LANES)
    )
    row_zero, row_two, row_one, row_three = call(
        functools.partial(split_kernel, row_count, halves),
        (rows_shape,) * row_count,
        [near_grads, wide_grads, chunk_sems],
        [pltpu.HBM],
    )(pltpu.with_memory_space_constraint(by_tile, pltpu.HBM))
    from_two = crossed(row_two, 2)
    from_one = crossed(row_one, 1)
    from_three = crossed(row_three, -1)
    slot_ids = owned_blocks.reshape(owners, slot_count).T
    block_ids = jnp.arange(block_total, dtype=jnp.int32)
    pick = (slot_ids[:, :, None] == block_ids[None, None, :]).astype(BF16)
    place = (slot_ids[:, None, :] == block_ids[None, :, None]).astype(BF16)
    row = jnp.arange(size_b, dtype=jnp.int32)[:, None]
    source = jnp.arange(owners, dtype=jnp.int32)[None, :]
    gather = (
        (row // row_count == source // copies) & (row % row_count == source % row_count)
    ).astype(BF16)
    outgoing = call(
        functools.partial(pick_kernel, halves), sent_shape, [wide_sent], [pltpu.VMEM] * 5
    )(pick, row_zero, from_two, from_one, from_three)
    owned_here = owned_blocks[shard_index, copy_index]
    row_limit = jnp.take(rows_valid, owned_here, mode="fill", fill_value=0)
    col_limit = jnp.take(cols_valid, owned_here, mode="fill", fill_value=0)
    limits = jnp.stack([row_limit, col_limit])
    outgoing, limits, gather = lax.optimization_barrier((outgoing, limits, gather))
    arrived = everywhere(outgoing)
    grad_block, parts_out = call(
        functools.partial(update_kernel, halves),
        (jax.ShapeDtypeStruct((slot_count, size_b, size_b), BF16), sent_shape),
        [wide_sent, wide_sent],
        [pltpu.SMEM] + [pltpu.VMEM] * 5,
    )(
        limits,
        gather,
        arrived,
        left_root[0, 0],
        right_root[0, 0],
        second_moment[0, 0],
    )
    returned = everywhere(parts_out)
    placed = call(
        functools.partial(place_kernel, halves), rows_shape, [wide_sent], [pltpu.VMEM] * 2
    )(place, returned)
    row_two = crossed(placed, 2)
    row_one = crossed(placed, 1)
    row_three = crossed(placed, -1)
    row_two, grad_block = lax.optimization_barrier((row_two, grad_block))
    left_next = factor_decay * left_factor[0, 0] + (1.0 - factor_decay) * jnp.einsum(
        "kij,klj->kil", grad_block, grad_block, preferred_element_type=F32
    )
    right_next = factor_decay * right_factor[0, 0] + (1.0 - factor_decay) * jnp.einsum(
        "kji,kjl->kil", grad_block, grad_block, preferred_element_type=F32
    )
    joined = call(
        functools.partial(join_kernel, row_count, halves),
        jax.ShapeDtypeStruct((tile_rows, LANES), BF16),
        [near_grads, wide_grads, chunk_sems],
        [pltpu.VMEM] * row_count,
        out_space=pltpu.HBM,
    )(placed, row_two, row_three, row_one)
    update = (
        joined.reshape(slab_count, tiles, row_count, LANES)
        .transpose(0, 2, 1, 3)
        .reshape(slab_count, row_count, col_count)
    )
    return (update, left_next[None, None], right_next[None, None])


def solution(mesh):
    in_specs = (
        P("rep", None, "fsdp", None),
        P(),
        P(),
        P(),
        P("fsdp", "rep", None, None, None),
        P("fsdp", "rep", None, None, None),
        P("fsdp", "rep", None, None, None),
        P("fsdp", "rep", None, None, None),
        P("fsdp", "rep", None, None, None),
    )
    out_specs = (
        P(None, "fsdp", None),
        P("fsdp", "rep", None, None, None),
        P("fsdp", "rep", None, None, None),
    )
    return jax.shard_map(body, mesh=mesh, in_specs=in_specs, out_specs=out_specs, check_vma=False)
```

```python
import functools

import jax
import jax.numpy as jnp
from jax import lax
from jax.experimental import pallas as pl
from jax.experimental.pallas import tpu as pltpu
from jax.sharding import PartitionSpec as P

factor_decay = 0.95
moment_decay = 0.999
adam_eps = 1e-08
LANES = 128
BF16 = jnp.bfloat16
F32 = jnp.float32


def call(kernel, out_shape, scratch_shapes, in_spaces, out_space=pltpu.VMEM, limit=32 * 1024 * 1024):
    return pl.pallas_call(
        kernel,
        out_shape=out_shape,
        in_specs=[pl.BlockSpec(memory_space=space) for space in in_spaces],
        out_specs=jax.tree.map(lambda _: pl.BlockSpec(memory_space=out_space), out_shape),
        scratch_shapes=list(scratch_shapes),
        compiler_params=pltpu.CompilerParams(vmem_limit_bytes=limit),
    )


def row_order(row_count):
    here = lax.axis_index("rep")
    turn = 2 * lax.rem(lax.axis_index("fsdp"), 2)
    return [lax.rem(here + by, row_count) for by in (0, 2, 1 + turn, 3 - turn)]


def split_kernel(row_count, halves, grads_ref, *refs):
    rows_at = row_order(row_count)
    outs, (near, wide, sems) = refs[:-3], refs[-3:]
    step = row_count * halves
    chunks = sems.shape[0]
    size = near.shape[0] // chunks
    copies = []
    for chunk in range(chunks):
        span = pl.ds(chunk * size, size)
        copy = pltpu.make_async_copy(grads_ref.at[span], near.at[span], sems.at[chunk])
        copy.start()
        copies.append(copy)
    for chunk, copy in enumerate(copies):
        copy.wait()
        first, last = chunk * size, (chunk + 1) * size
        wide[first:last, :] = near[first:last, :].astype(F32)
        for n, out in enumerate(outs):
            for half in range(halves):
                start = first + half * row_count + rows_at[n]
                part = wide[pl.ds(start, size // step, stride=step), :]
                out[first // step : last // step, half * LANES : (half + 1) * LANES] = part.astype(
                    BF16
                )


def join_kernel(row_count, halves, *refs):
    rows_at = row_order(row_count)
    ins, (out_ref, near, wide, sems) = refs[:row_count], refs[row_count:]
    step = row_count * halves
    chunks = sems.shape[0]
    size = near.shape[0] // chunks
    copies = []
    for chunk in range(chunks):
        first, last = chunk * size, (chunk + 1) * size
        for n, rows in enumerate(ins):
            for half in range(halves):
                start = first + half * row_count + rows_at[n]
                part = rows[first // step : last // step, half * LANES : (half + 1) * LANES]
                wide[pl.ds(start, size // step, stride=step), :] = part.astype(F32)
        near[first:last, :] = wide[first:last, :].astype(BF16)
        span = pl.ds(first, size)
        copy = pltpu.make_async_copy(near.at[span], out_ref.at[span], sems.at[chunk])
        copy.start()
        copies.append(copy)
    for copy in copies:
        copy.wait()


def pick_kernel(halves, pick_ref, own_ref, two_ref, one_ref, three_ref, out_ref, wide):
    slots, owners = pick_ref.shape[:2]
    total = (
        own_ref[...].astype(F32)
        + one_ref[...].astype(F32)
        + two_ref[...].astype(F32)
        + three_ref[...].astype(F32)
    ).astype(BF16)
    for slot in range(slots):
        rows = jnp.dot(pick_ref[slot], total, preferred_element_type=F32)
        for half in range(halves):
            wide[pl.ds(half * slots + slot, owners, stride=halves * slots), :] = rows[
                :, half * LANES : (half + 1) * LANES
            ]
    out_ref[...] = wide[: out_ref.shape[0], :].astype(BF16)


def place_kernel(halves, place_ref, got_ref, out_ref, wide):
    slots, _, owners = place_ref.shape
    wide[: got_ref.shape[0], :] = got_ref[...].astype(F32)
    rows = 0.0
    for slot in range(slots):
        parts = [
            wide[pl.ds(half * slots + slot, owners, stride=halves * slots), :].astype(BF16)
            for half in range(halves)
        ]
        rows = rows + jnp.dot(
            place_ref[slot], jnp.concatenate(parts, axis=1), preferred_element_type=F32
        )
    out_ref[...] = rows.astype(BF16)


def update_kernel(
    halves, limits_ref, gather_ref, got_ref, lroot_ref, rroot_ref, moment_ref,
    grad_ref, out_ref, wide, wide_out,
):
    slots, size = grad_ref.shape[:2]
    owners = gather_ref.shape[1]
    step = slots * halves
    every = range(slots)
    wide[: got_ref.shape[0], :] = got_ref[...].astype(F32)
    row_ids = lax.broadcasted_iota(jnp.int32, (size, size), 0)
    col_ids = lax.broadcasted_iota(jnp.int32, (size, size), 1)
    parts = [
        wide[pl.ds(half * slots + slot, owners, stride=step), :].astype(BF16)
        for slot in every
        for half in range(halves)
    ]
    blocks = jnp.dot(
        gather_ref[...], jnp.concatenate(parts, axis=1), preferred_element_type=F32
    ).astype(BF16)
    inside, wides, grads = [], [], []
    for slot in every:
        inside.append((row_ids < limits_ref[0, slot]) & (col_ids < limits_ref[1, slot]))
        block = blocks[:, slot * size : (slot + 1) * size].astype(F32)
        wides.append(jnp.where(inside[slot], block, 0.0))
        grads.append(wides[slot].astype(BF16))
        grad_ref[slot] = grads[slot]
    halfway = [
        jnp.dot(lroot_ref[slot], grads[slot], preferred_element_type=F32).astype(BF16)
        for slot in every
    ]
    preconds = [
        jnp.where(
            inside[slot], jnp.dot(halfway[slot], rroot_ref[slot], preferred_element_type=F32), 0.0
        )
        for slot in every
    ]
    updates = []
    for slot, (grad_wide, precond) in enumerate(zip(wides, preconds)):
        moment = moment_decay * moment_ref[slot] + (1.0 - moment_decay) * grad_wide * grad_wide
        adam = grad_wide / (jnp.sqrt(moment) + adam_eps)
        adam_norm = jnp.sqrt(jnp.sum(adam * adam, axis=(0, 1), keepdims=True))
        pre_norm = jnp.sqrt(jnp.sum(precond * precond, axis=(0, 1), keepdims=True) + 1e-06)
        updates.append((precond * (adam_norm / pre_norm)).astype(BF16))
    rows = lax.dot_general(
        gather_ref[...],
        jnp.concatenate(updates, axis=1),
        (((0,), (0,)), ((), ())),
        preferred_element_type=F32,
    )
    for slot in every:
        for half in range(halves):
            first = slot * size + half * LANES
            wide_out[pl.ds(half * slots + slot, owners, stride=step), :] = rows[
                :, first : first + LANES
            ]
    out_ref[...] = wide_out[: out_ref.shape[0], :].astype(BF16)


def factor_kernel(grad_ref, left_ref, right_ref, left_out, right_out, left, right, sems):
    copies = []
    for slot in range(grad_ref.shape[0]):
        grad = grad_ref[slot]
        for side, (old, new, out) in enumerate(
            ((left_ref, left, left_out), (right_ref, right, right_out))
        ):
            product = lax.dot_general(
                grad, grad, (((1 - side,), (1 - side,)), ((), ())), preferred_element_type=F32
            )
            new[slot] = factor_decay * old[slot] + (1.0 - factor_decay) * product
            copy = pltpu.make_async_copy(new.at[slot], out.at[slot], sems.at[2 * slot + side])
            copy.start()
            copies.append(copy)
    for copy in copies:
        copy.wait()


def body(
    gradients,
    owned_blocks,
    rows_valid,
    cols_valid,
    left_factor,
    right_factor,
    left_root,
    right_root,
    second_moment,
):
    shards = lax.axis_size("fsdp")
    copies = lax.axis_size("rep")
    owners = shards * copies
    shard_index = lax.axis_index("fsdp")
    copy_index = lax.axis_index("rep")
    slab_count, row_count, col_count = gradients.shape[1:]
    size_b = left_factor.shape[-1]
    slot_count = owned_blocks.shape[2]
    block_total = slab_count * (col_count // size_b)
    halves = size_b // LANES
    tiles = col_count // LANES
    def crossed(operand, by):
        pairs = []
        for owner in range(shards):
            step = by if owner % 2 == 0 else -by
            pairs += [
                (owner * copies + i, owner * copies + (i + step) % copies) for i in range(copies)
            ]
        return lax.ppermute(operand, ("fsdp", "rep"), pairs)

    def everywhere(operand):
        return lax.all_to_all(operand, ("fsdp", "rep"), split_axis=0, concat_axis=0, tiled=True)

    rows_shape = jax.ShapeDtypeStruct((block_total, size_b), BF16)
    sent_shape = jax.ShapeDtypeStruct((owners * halves * slot_count, LANES), BF16)
    tile_rows = slab_count * tiles * row_count
    near_grads = pltpu.VMEM((tile_rows, LANES), BF16)
    wide_grads = pltpu.VMEM((tile_rows + row_count * halves, LANES), F32)
    chunk_sems = pltpu.SemaphoreType.DMA((8,))
    wide_sent = pltpu.VMEM((sent_shape.shape[0] + 8, LANES), F32)

    by_tile = (
        gradients[0]
        .reshape(slab_count, row_count, tiles, LANES)
        .transpose(0, 2, 1, 3)
        .reshape(tile_rows, LANES)
    )
    row_zero, row_two, row_one, row_three = call(
        functools.partial(split_kernel, row_count, halves),
        (rows_shape,) * row_count,
        [near_grads, wide_grads, chunk_sems],
        [pltpu.HBM],
    )(pltpu.with_memory_space_constraint(by_tile, pltpu.HBM))
    from_two = crossed(row_two, 2)
    from_one = crossed(row_one, 1)
    from_three = crossed(row_three, -1)
    slot_ids = owned_blocks.reshape(owners, slot_count).T
    block_ids = jnp.arange(block_total, dtype=jnp.int32)
    pick = (slot_ids[:, :, None] == block_ids[None, None, :]).astype(BF16)
    place = (slot_ids[:, None, :] == block_ids[None, :, None]).astype(BF16)
    row = jnp.arange(size_b, dtype=jnp.int32)[:, None]
    source = jnp.arange(owners, dtype=jnp.int32)[None, :]
    gather = (
        (row // row_count == source // copies) & (row % row_count == source % row_count)
    ).astype(BF16)
    outgoing = call(
        functools.partial(pick_kernel, halves), sent_shape, [wide_sent], [pltpu.VMEM] * 5
    )(pick, row_zero, from_two, from_one, from_three)
    owned_here = owned_blocks[shard_index, copy_index]
    row_limit = jnp.take(rows_valid, owned_here, mode="fill", fill_value=0)
    col_limit = jnp.take(cols_valid, owned_here, mode="fill", fill_value=0)
    limits = jnp.stack([row_limit, col_limit])
    outgoing, limits, gather = lax.optimization_barrier((outgoing, limits, gather))
    arrived = everywhere(outgoing)
    grad_block, parts_out = call(
        functools.partial(update_kernel, halves),
        (jax.ShapeDtypeStruct((slot_count, size_b, size_b), BF16), sent_shape),
        [wide_sent, wide_sent],
        [pltpu.SMEM] + [pltpu.VMEM] * 5,
    )(
        limits,
        gather,
        arrived,
        left_root[0, 0],
        right_root[0, 0],
        second_moment[0, 0],
    )
    returned = everywhere(parts_out)
    placed = call(
        functools.partial(place_kernel, halves), rows_shape, [wide_sent], [pltpu.VMEM] * 2
    )(place, returned)
    row_two = crossed(placed, 2)
    row_one = crossed(placed, 1)
    row_three = crossed(placed, -1)
    row_two, grad_block = lax.optimization_barrier((row_two, grad_block))
    factors_shape = jax.ShapeDtypeStruct((slot_count, size_b, size_b), F32)
    factors_scratch = pltpu.VMEM((slot_count, size_b, size_b), F32)
    left_next, right_next = call(
        factor_kernel,
        (factors_shape, factors_shape),
        [factors_scratch, factors_scratch, pltpu.SemaphoreType.DMA((2 * slot_count,))],
        [pltpu.VMEM] * 3,
        out_space=pltpu.HBM,
    )(grad_block, left_factor[0, 0], right_factor[0, 0])
    joined = call(
        functools.partial(join_kernel, row_count, halves),
        jax.ShapeDtypeStruct((tile_rows, LANES), BF16),
        [near_grads, wide_grads, chunk_sems],
        [pltpu.VMEM] * row_count,
        out_space=pltpu.HBM,
    )(placed, row_two, row_three, row_one)
    update = (
        joined.reshape(slab_count, tiles, row_count, LANES)
        .transpose(0, 2, 1, 3)
        .reshape(slab_count, row_count, col_count)
    )
    return (update, left_next[None, None], right_next[None, None])


def solution(mesh):
    in_specs = (
        P("rep", None, "fsdp", None),
        P(),
        P(),
        P(),
        P("fsdp", "rep", None, None, None),
        P("fsdp", "rep", None, None, None),
        P("fsdp", "rep", None, None, None),
        P("fsdp", "rep", None, None, None),
        P("fsdp", "rep", None, None, None),
    )
    out_specs = (
        P(None, "fsdp", None),
        P("fsdp", "rep", None, None, None),
        P("fsdp", "rep", None, None, None),
    )
    return jax.shard_map(body, mesh=mesh, in_specs=in_specs, out_specs=out_specs, check_vma=False)
```

```python
import functools

import jax
import jax.numpy as jnp
from jax import lax
from jax.experimental import pallas as pl
from jax.experimental.pallas import tpu as pltpu
from jax.sharding import PartitionSpec as P

factor_decay = 0.95
moment_decay = 0.999
adam_eps = 1e-08
LANES = 128
BF16 = jnp.bfloat16
F32 = jnp.float32


def call(kernel, out_shape, scratch_shapes, in_spaces, out_space=pltpu.VMEM, limit=32 * 1024 * 1024):
    return pl.pallas_call(
        kernel,
        out_shape=out_shape,
        in_specs=[pl.BlockSpec(memory_space=space) for space in in_spaces],
        out_specs=jax.tree.map(lambda _: pl.BlockSpec(memory_space=out_space), out_shape),
        scratch_shapes=list(scratch_shapes),
        compiler_params=pltpu.CompilerParams(vmem_limit_bytes=limit),
    )


def row_order(row_count):
    here = lax.axis_index("rep")
    turn = 2 * lax.rem(lax.axis_index("fsdp"), 2)
    return [lax.rem(here + by, row_count) for by in (0, 2, 1 + turn, 3 - turn)]


def split_kernel(row_count, halves, grads_ref, *refs):
    rows_at = row_order(row_count)
    outs, (near, wide, sems) = refs[:-3], refs[-3:]
    step = row_count * halves
    chunks = sems.shape[0]
    size = near.shape[0] // chunks
    copies = []
    for chunk in range(chunks):
        span = pl.ds(chunk * size, size)
        copy = pltpu.make_async_copy(grads_ref.at[span], near.at[span], sems.at[chunk])
        copy.start()
        copies.append(copy)
    for chunk, copy in enumerate(copies):
        copy.wait()
        first, last = chunk * size, (chunk + 1) * size
        wide[first:last, :] = near[first:last, :].astype(F32)
        for n, out in enumerate(outs):
            for half in range(halves):
                start = first + half * row_count + rows_at[n]
                part = wide[pl.ds(start, size // step, stride=step), :]
                out[first // step : last // step, half * LANES : (half + 1) * LANES] = part.astype(
                    BF16
                )


def join_kernel(row_count, halves, *refs):
    rows_at = row_order(row_count)
    ins, (out_ref, near, wide, sems) = refs[:row_count], refs[row_count:]
    step = row_count * halves
    chunks = sems.shape[0]
    size = near.shape[0] // chunks
    copies = []
    for chunk in range(chunks):
        first, last = chunk * size, (chunk + 1) * size
        for n, rows in enumerate(ins):
            for half in range(halves):
                start = first + half * row_count + rows_at[n]
                part = rows[first // step : last // step, half * LANES : (half + 1) * LANES]
                wide[pl.ds(start, size // step, stride=step), :] = part.astype(F32)
        near[first:last, :] = wide[first:last, :].astype(BF16)
        span = pl.ds(first, size)
        copy = pltpu.make_async_copy(near.at[span], out_ref.at[span], sems.at[chunk])
        copy.start()
        copies.append(copy)
    for copy in copies:
        copy.wait()


def pick_kernel(halves, pick_ref, own_ref, two_ref, one_ref, three_ref, out_ref, wide):
    slots, owners = pick_ref.shape[:2]
    total = (
        own_ref[...].astype(F32)
        + one_ref[...].astype(F32)
        + two_ref[...].astype(F32)
        + three_ref[...].astype(F32)
    ).astype(BF16)
    for slot in range(slots):
        rows = jnp.dot(pick_ref[slot], total, preferred_element_type=F32)
        for half in range(halves):
            wide[pl.ds(half * slots + slot, owners, stride=halves * slots), :] = rows[
                :, half * LANES : (half + 1) * LANES
            ]
    out_ref[...] = wide[: out_ref.shape[0], :].astype(BF16)


def place_kernel(halves, place_ref, got_ref, out_ref, wide):
    slots, _, owners = place_ref.shape
    wide[: got_ref.shape[0], :] = got_ref[...].astype(F32)
    rows = 0.0
    for slot in range(slots):
        parts = [
            wide[pl.ds(half * slots + slot, owners, stride=halves * slots), :].astype(BF16)
            for half in range(halves)
        ]
        rows = rows + jnp.dot(
            place_ref[slot], jnp.concatenate(parts, axis=1), preferred_element_type=F32
        )
    out_ref[...] = rows.astype(BF16)


def update_kernel(
    halves, limits_ref, gather_ref, got_ref, lroot_ref, rroot_ref, moment_ref,
    grad_ref, out_ref, wide, wide_out,
):
    slots, size = grad_ref.shape[:2]
    owners = gather_ref.shape[1]
    step = slots * halves
    every = range(slots)
    wide[: got_ref.shape[0], :] = got_ref[...].astype(F32)
    row_ids = lax.broadcasted_iota(jnp.int32, (size, size), 0)
    col_ids = lax.broadcasted_iota(jnp.int32, (size, size), 1)
    parts = [
        wide[pl.ds(half * slots + slot, owners, stride=step), :].astype(BF16)
        for slot in every
        for half in range(halves)
    ]
    blocks = jnp.dot(
        gather_ref[...], jnp.concatenate(parts, axis=1), preferred_element_type=F32
    ).astype(BF16)
    inside, wides, grads = [], [], []
    for slot in every:
        inside.append((row_ids < limits_ref[0, slot]) & (col_ids < limits_ref[1, slot]))
        block = blocks[:, slot * size : (slot + 1) * size].astype(F32)
        wides.append(jnp.where(inside[slot], block, 0.0))
        grads.append(wides[slot].astype(BF16))
        grad_ref[slot] = grads[slot]
    adam_norms = []
    for slot, grad_wide in enumerate(wides):
        moment = moment_decay * moment_ref[slot] + (1.0 - moment_decay) * grad_wide * grad_wide
        adam = grad_wide / (jnp.sqrt(moment) + adam_eps)
        adam_norms.append(jnp.sqrt(jnp.sum(adam * adam, axis=(0, 1), keepdims=True)))
    halfway = [
        jnp.dot(lroot_ref[slot], grads[slot], preferred_element_type=F32).astype(BF16)
        for slot in every
    ]
    preconds = [
        jnp.where(
            inside[slot], jnp.dot(halfway[slot], rroot_ref[slot], preferred_element_type=F32), 0.0
        )
        for slot in every
    ]
    updates = []
    for adam_norm, precond in zip(adam_norms, preconds):
        pre_norm = jnp.sqrt(jnp.sum(precond * precond, axis=(0, 1), keepdims=True) + 1e-06)
        updates.append((precond * (adam_norm / pre_norm)).astype(BF16))
    rows = lax.dot_general(
        gather_ref[...],
        jnp.concatenate(updates, axis=1),
        (((0,), (0,)), ((), ())),
        preferred_element_type=F32,
    )
    for slot in every:
        for half in range(halves):
            first = slot * size + half * LANES
            wide_out[pl.ds(half * slots + slot, owners, stride=step), :] = rows[
                :, first : first + LANES
            ]
    out_ref[...] = wide_out[: out_ref.shape[0], :].astype(BF16)


def factor_kernel(grad_ref, left_ref, right_ref, left_out, right_out, left, right, sems):
    copies = []
    for slot in range(grad_ref.shape[0]):
        grad = grad_ref[slot]
        for side, (old, new, out) in enumerate(
            ((left_ref, left, left_out), (right_ref, right, right_out))
        ):
            product = lax.dot_general(
                grad, grad, (((1 - side,), (1 - side,)), ((), ())), preferred_element_type=F32
            )
            new[slot] = factor_decay * old[slot] + (1.0 - factor_decay) * product
            copy = pltpu.make_async_copy(new.at[slot], out.at[slot], sems.at[2 * slot + side])
            copy.start()
            copies.append(copy)
    for copy in copies:
        copy.wait()


def body(
    gradients,
    owned_blocks,
    rows_valid,
    cols_valid,
    left_factor,
    right_factor,
    left_root,
    right_root,
    second_moment,
):
    shards = lax.axis_size("fsdp")
    copies = lax.axis_size("rep")
    owners = shards * copies
    shard_index = lax.axis_index("fsdp")
    copy_index = lax.axis_index("rep")
    slab_count, row_count, col_count = gradients.shape[1:]
    size_b = left_factor.shape[-1]
    slot_count = owned_blocks.shape[2]
    block_total = slab_count * (col_count // size_b)
    halves = size_b // LANES
    tiles = col_count // LANES
    def crossed(operand, by):
        pairs = []
        for owner in range(shards):
            step = by if owner % 2 == 0 else -by
            pairs += [
                (owner * copies + i, owner * copies + (i + step) % copies) for i in range(copies)
            ]
        return lax.ppermute(operand, ("fsdp", "rep"), pairs)

    def everywhere(operand):
        return lax.all_to_all(operand, ("fsdp", "rep"), split_axis=0, concat_axis=0, tiled=True)

    rows_shape = jax.ShapeDtypeStruct((block_total, size_b), BF16)
    sent_shape = jax.ShapeDtypeStruct((owners * halves * slot_count, LANES), BF16)
    tile_rows = slab_count * tiles * row_count
    near_grads = pltpu.VMEM((tile_rows, LANES), BF16)
    wide_grads = pltpu.VMEM((tile_rows + row_count * halves, LANES), F32)
    chunk_sems = pltpu.SemaphoreType.DMA((8,))
    wide_sent = pltpu.VMEM((sent_shape.shape[0] + 8, LANES), F32)

    by_tile = (
        gradients[0]
        .reshape(slab_count, row_count, tiles, LANES)
        .transpose(0, 2, 1, 3)
        .reshape(tile_rows, LANES)
    )
    row_zero, row_two, row_one, row_three = call(
        functools.partial(split_kernel, row_count, halves),
        (rows_shape,) * row_count,
        [near_grads, wide_grads, chunk_sems],
        [pltpu.HBM],
    )(pltpu.with_memory_space_constraint(by_tile, pltpu.HBM))
    from_two = crossed(row_two, 2)
    from_one = crossed(row_one, 1)
    from_three = crossed(row_three, -1)
    slot_ids = owned_blocks.reshape(owners, slot_count).T
    block_ids = jnp.arange(block_total, dtype=jnp.int32)
    pick = (slot_ids[:, :, None] == block_ids[None, None, :]).astype(BF16)
    place = (slot_ids[:, None, :] == block_ids[None, :, None]).astype(BF16)
    row = jnp.arange(size_b, dtype=jnp.int32)[:, None]
    source = jnp.arange(owners, dtype=jnp.int32)[None, :]
    gather = (
        (row // row_count == source // copies) & (row % row_count == source % row_count)
    ).astype(BF16)
    outgoing = call(
        functools.partial(pick_kernel, halves), sent_shape, [wide_sent], [pltpu.VMEM] * 5
    )(pick, row_zero, from_two, from_one, from_three)
    owned_here = owned_blocks[shard_index, copy_index]
    row_limit = jnp.take(rows_valid, owned_here, mode="fill", fill_value=0)
    col_limit = jnp.take(cols_valid, owned_here, mode="fill", fill_value=0)
    limits = jnp.stack([row_limit, col_limit])
    outgoing, limits, gather = lax.optimization_barrier((outgoing, limits, gather))
    arrived = everywhere(outgoing)
    grad_block, parts_out = call(
        functools.partial(update_kernel, halves),
        (jax.ShapeDtypeStruct((slot_count, size_b, size_b), BF16), sent_shape),
        [wide_sent, wide_sent],
        [pltpu.SMEM] + [pltpu.VMEM] * 5,
    )(
        limits,
        gather,
        arrived,
        left_root[0, 0],
        right_root[0, 0],
        second_moment[0, 0],
    )
    returned = everywhere(parts_out)
    placed = call(
        functools.partial(place_kernel, halves), rows_shape, [wide_sent], [pltpu.VMEM] * 2
    )(place, returned)
    row_two = crossed(placed, 2)
    row_one = crossed(placed, 1)
    row_three = crossed(placed, -1)
    row_two, grad_block = lax.optimization_barrier((row_two, grad_block))
    factors_shape = jax.ShapeDtypeStruct((slot_count, size_b, size_b), F32)
    factors_scratch = pltpu.VMEM((slot_count, size_b, size_b), F32)
    left_next, right_next = call(
        factor_kernel,
        (factors_shape, factors_shape),
        [factors_scratch, factors_scratch, pltpu.SemaphoreType.DMA((2 * slot_count,))],
        [pltpu.VMEM] * 3,
        out_space=pltpu.HBM,
    )(grad_block, left_factor[0, 0], right_factor[0, 0])
    joined = call(
        functools.partial(join_kernel, row_count, halves),
        jax.ShapeDtypeStruct((tile_rows, LANES), BF16),
        [near_grads, wide_grads, chunk_sems],
        [pltpu.VMEM] * row_count,
        out_space=pltpu.HBM,
    )(placed, row_two, row_three, row_one)
    update = (
        joined.reshape(slab_count, tiles, row_count, LANES)
        .transpose(0, 2, 1, 3)
        .reshape(slab_count, row_count, col_count)
    )
    return (update, left_next[None, None], right_next[None, None])


def solution(mesh):
    in_specs = (
        P("rep", None, "fsdp", None),
        P(),
        P(),
        P(),
        P("fsdp", "rep", None, None, None),
        P("fsdp", "rep", None, None, None),
        P("fsdp", "rep", None, None, None),
        P("fsdp", "rep", None, None, None),
        P("fsdp", "rep", None, None, None),
    )
    out_specs = (
        P(None, "fsdp", None),
        P("fsdp", "rep", None, None, None),
        P("fsdp", "rep", None, None, None),
    )
    return jax.shard_map(body, mesh=mesh, in_specs=in_specs, out_specs=out_specs, check_vma=False)
```
